128 devices in a mesh: span: 4 (over y_lo, core), tm: 32 (over z, y_hi, x).
Axes of the slice: x: 4, y: 4 (y_hi: 2, y_lo: 2; y = y_hi * 2 + y_lo), z: 4, core: 2. Of those that a mesh axis runs over, the one named last changes fastest.
Arguments:
- window_start: int32 [1], replicated, may hold values from 0 to 3968
- owner_map: int32 [32], replicated, may hold values from 0 to 31, each once
- core: bfloat16 [3, 512, 384, 192], P(None, 'tm', 'span'), may hold values from -6 to 6
- span_factor: bfloat16 [1024, 384], P('span'), may hold values from -0.3125 to 0.3125
- height_factor: bfloat16 [512, 192], replicated, may hold values from -0.4375 to 0.4375
- time_factor: bfloat16 [4096, 512], P(None, 'tm'), may hold values from -0.25 to 0.25
Outputs:
- inlet: bfloat16 [128, 3, 1024, 512], P(None, None, ('span', 'tm'))
The draws below stay inside these ranges and needn't reach their ends.
Inputs may be any that keep to these rules, and one draw needn't show every extreme that they name: owner_map holds each of 0 to 31 once.
All inputs are finite; a program needn't handle non-finite values.
Results may differ from the reference program's by a relative error of at most 0.0058.
Values may be sent and summed in bfloat16 or wider, within the bound.
No kernel may reach another device: no remote copies, remote signals or barrier semaphores. Data moves between devices by JAX's collectives and lax.ppermute only.
A program may use at most 192 MiB of HBM per device.

```python
import jax
import jax.numpy as jnp
from jax import lax

C = 3
R1 = 384
R2 = 192
R3 = 512
SPAN = 1024
H = 512
TT = 4096
PL_DEV = 4
N_SPAN = 4
N_TM = 32


def shard_levels(key, extent, cuts, least, high):
    level = 1.0
    for position, blocks in cuts:
        steps = jax.random.uniform(jax.random.fold_in(jax.random.fold_in(key, 6), position), (blocks,), jnp.float32, least / len(cuts), high / len(cuts))
        level = level * jnp.repeat(jnp.exp(steps), extent[position] // blocks).reshape((-1,) + (1,) * (len(extent) - 1 - position))
    return level


def scatter_about(rng, dims, scale, limit, pieces=(), kind=jnp.bfloat16):
    drawn = jax.random.normal(rng, dims, jnp.float32) * scale
    if len(pieces) > 0:
        drawn = shard_levels(rng, dims, pieces, -0.22, 0.18) * drawn
    return jnp.clip(drawn, min=-limit, max=limit).astype(kind)


def setup_inputs(seed: int = 0) -> dict:
    key_list = jax.random.split(jax.random.key(seed), 7)
    window_start = jax.random.randint(key_list[0], (1,), 0, TT - PL_DEV * N_TM + 1).astype(jnp.int32)
    owner_map = jax.random.permutation(key_list[1], N_TM).astype(jnp.int32)
    core = scatter_about(key_list[2], (C, R3, R1, R2), 1.0, 6.0, ((1, 32), (2, 4)))
    span_factor = scatter_about(key_list[3], (SPAN, R1), R1 ** -0.5, 0.3125, ((0, 4),))
    height_factor = scatter_about(key_list[4], (H, R2), R2 ** -0.5, 0.4375)
    time_factor = scatter_about(key_list[5], (TT, R3), R3 ** -0.5, 0.25, ((1, 32),))
    return dict(window_start=window_start, owner_map=owner_map, core=core, span_factor=span_factor, height_factor=height_factor, time_factor=time_factor)


def reference(window_start, owner_map, core, span_factor, height_factor, time_factor):
    count = PL_DEV * N_TM
    rows = lax.dynamic_slice_in_dim(time_factor, window_start[0].astype(jnp.int32), count, 0)
    core_wide = core.astype(jnp.float32)
    height_wide = height_factor.astype(jnp.float32)
    span_wide = span_factor.astype(jnp.float32)
    high = lax.Precision.HIGHEST

    def one_plane(row):
        first = jnp.einsum('r,crab->cab', row.astype(jnp.float32), core_wide, precision=high)
        first = first.astype(jnp.bfloat16).astype(jnp.float32)
        second = jnp.einsum('cab,hb->cah', first, height_wide, precision=high)
        second = second.astype(jnp.bfloat16).astype(jnp.float32)
        return jnp.einsum('sa,cah->csh', span_wide, second, precision=high).astype(jnp.bfloat16)

    planes = lax.map(one_plane, rows)
    tiles = jnp.arange(N_TM, dtype=jnp.int32)
    owned = jnp.sum(jnp.where(owner_map[:, None] == tiles[None, :], tiles[:, None], 0), axis=0).astype(jnp.int32)
    tile_rows = SPAN // (N_SPAN * N_TM)
    blocks = planes.reshape(count, C, N_SPAN, N_TM, tile_rows, H)
    blocks = jnp.take(blocks, owned, axis=3)
    return blocks.reshape(count, C, SPAN, H)
```

```python
import jax
import jax.numpy as jnp
from jax import lax
from jax.experimental import pallas as pl
from jax.experimental.pallas import tpu as pltpu
from jax.sharding import PartitionSpec as P

AXES = ("span", "tm")
PLANES = 128
DEV = 128
TM = 32
SPAN_DEV = 4
R_LOC = 16
A_LOC = 96
HALF = A_LOC // 2
B = 192
SEND1 = 72
SEND2 = 40
F32 = jnp.float32
BF16 = jnp.bfloat16
LIMIT = pltpu.CompilerParams(vmem_limit_bytes=48 * 1024 * 1024)
VMEM = pl.BlockSpec(memory_space=pltpu.VMEM)


def deal_kernel(core_ref, rows_ref, out_ref, turned):
    eye = (
        lax.broadcasted_iota(jnp.int32, (B, B), 0) == lax.broadcasted_iota(jnp.int32, (B, B), 1)
    ).astype(BF16)
    lane = lax.broadcasted_iota(jnp.int32, (1, 1, 128), 2)
    rows = rows_ref[...].astype(F32)
    turned[...] = jnp.zeros_like(turned)
    for c in range(3):
        for r in range(R_LOC):
            turned[:, r, :A_LOC] = lax.dot_general(
                eye, core_ref[c, r], (((1,), (1,)), ((), ())), preferred_element_type=F32
            )
        full = B if c < 2 else B - 64
        blocks = full // 4
        first = c * (B // 4)

        def put(i, carry, first=first):
            for q in range(4):
                block = jnp.where(lane[0] < A_LOC, turned[4 * i + q], rows[q])
                out_ref[first + i, R_LOC * q : R_LOC * (q + 1), :] = block.astype(BF16)
            return carry

        lax.fori_loop(0, blocks, put, 0, unroll=4)
    low = turned[128:, :8, :]
    high = turned[128:, 8:, :]
    at_0 = jnp.where(lane < HALF, low, pltpu.roll(high, HALF, 2))
    at_1 = jnp.where(lane < HALF, pltpu.roll(low, 128 - HALF, 2), high)

    both = jnp.concatenate([at_0[:, None], at_1[:, None]], axis=1).reshape(DEV, 8, 128)
    out_ref[:, 64:, :] = both.astype(BF16)


def middle_kernel(got_ref, span_ref, out_ref, firsts):
    lane = lax.broadcasted_iota(jnp.int32, (1, 1, 128), 2)
    lane2 = lane[0]
    w = jnp.zeros((TM, R_LOC, 128), F32)
    for q in range(4):
        piece = got_ref[:TM, R_LOC * q : R_LOC * (q + 1), :].astype(F32)
        piece = pltpu.roll(piece, (32 * q - 96) % 128, 2)
        w = jnp.where((lane >= 32 * q) & (lane < 32 * q + 32), piece, w)
    whole = w.reshape(TM * R_LOC, 128).T.astype(BF16)
    low = w[:, :8].reshape(TM * 8, 128).T.astype(BF16)
    high = w[:, 8:].reshape(TM * 8, 128).T.astype(BF16)
    odd = lax.rem(lax.axis_index("tm"), 2) == 1
    for g in range(SPAN_DEV):
        at = slice(g * 128, (g + 1) * 128)
        for q in range(4):
            x = got_ref[TM * g : TM * (g + 1), R_LOC * q : R_LOC * (q + 1), :].reshape(TM * R_LOC, 128)
            firsts[q, :, at] = jnp.dot(whole, x, preferred_element_type=F32).astype(BF16)
        x = got_ref[TM * g : TM * (g + 1), 64:, :].astype(F32).reshape(TM * 8, 128).astype(BF16)
        fa = jnp.dot(low, x, preferred_element_type=F32)
        fb = jnp.dot(high, x, preferred_element_type=F32)
        even_sum = jnp.where(lane2 < HALF, fa + pltpu.roll(fb, 128 - HALF, 1), 0.0)
        odd_sum = jnp.where((lane2 >= HALF) & (lane2 < A_LOC), pltpu.roll(fa, HALF, 1) + fb, 0.0)
        firsts[4, :, at] = jnp.where(odd, odd_sum, even_sum).astype(BF16)
    for q in range(5):
        z = lax.dot_general(
            span_ref[...], firsts[q], (((1,), (1,)), ((), ())), preferred_element_type=F32
        )
        out_ref[:, 8 * q : 8 * (q + 1), :] = z.reshape(DEV, 8, 128).astype(BF16)


def height_kernel(got_ref, height_ref, tail_ref, out_ref, wide, rows):
    for c in range(3):
        if c < 2:
            x = got_ref[48 * c : 48 * (c + 1), :32, :].astype(F32)
            wide[:B] = x.reshape(B, 8, 128)
            depth = B
            factor = height_ref[...]
        else:
            wide[:128] = got_ref[96:, :32, :].astype(F32).reshape(128, 8, 128)
            wide[128:] = got_ref[:, 32:, :].astype(F32)
            depth = 256
            factor = tail_ref[...]
        for s in range(8):
            rows[:, s, :depth] = wide[:depth, s, :].T
        x = rows[:, :, :depth].reshape(PLANES * 8, depth).astype(BF16)
        y = jnp.dot(x, factor, preferred_element_type=F32)
        out_ref[:, c] = y.reshape(PLANES, 8, 512).astype(BF16)


def body(window_start, owner_map, core, span_factor, height_factor, time_factor):
    rows = lax.dynamic_slice_in_dim(time_factor, window_start[0], PLANES, 0)
    quarters = jnp.pad(rows.T.reshape(R_LOC, 4, 32).transpose(1, 0, 2), ((0, 0), (0, 0), (A_LOC, 0)))
    sent = pl.pallas_call(
        deal_kernel,
        out_shape=jax.ShapeDtypeStruct((DEV, SEND1, 128), BF16),
        in_specs=[VMEM, VMEM],
        out_specs=VMEM,
        scratch_shapes=[pltpu.VMEM((B, R_LOC, 128), F32)],
        compiler_params=LIMIT,
        name="deal",
    )(core, quarters)
    got = lax.all_to_all(sent, AXES, 0, 0, tiled=True)

    tiles = jnp.arange(TM, dtype=jnp.int32)
    owned = jnp.sum(jnp.where(owner_map[:, None] == tiles[None, :], tiles[:, None], 0), axis=0)
    span = jnp.take(span_factor.reshape(TM, 8, SPAN_DEV * A_LOC), owned, axis=0)
    span = lax.all_gather(span.reshape(TM * 8, SPAN_DEV * A_LOC), "span", axis=0, tiled=True)
    span = jnp.pad(span.reshape(8 * DEV, SPAN_DEV, A_LOC), ((0, 0), (0, 0), (0, 128 - A_LOC)))
    span = span.reshape(8 * DEV, SPAN_DEV * 128)

    sent = pl.pallas_call(
        middle_kernel,
        out_shape=jax.ShapeDtypeStruct((DEV, SEND2, 128), BF16),
        in_specs=[VMEM, VMEM],
        out_specs=VMEM,
        scratch_shapes=[pltpu.VMEM((5, PLANES, SPAN_DEV * 128), BF16)],
        compiler_params=LIMIT,
        name="middle",
    )(got, span)
    got = lax.all_to_all(sent, AXES, 0, 0, tiled=True)

    height = height_factor.T
    tail = jnp.concatenate([height[:128], jnp.repeat(height[128:], 2, axis=0)], axis=0)
    return pl.pallas_call(
        height_kernel,
        out_shape=jax.ShapeDtypeStruct((PLANES, 3, 8, 512), BF16),
        in_specs=[VMEM, VMEM, VMEM],
        out_specs=VMEM,
        scratch_shapes=[pltpu.VMEM((256, 8, 128), F32), pltpu.VMEM((PLANES, 8, 256), F32)],
        compiler_params=LIMIT,
        name="height",
    )(got, height, tail)


def solution(mesh):
    in_specs = (P(), P(), P(None, "tm", "span", None), P("span", None), P(), P(None, "tm"))
    out_specs = P(None, None, ("span", "tm"), None)
    return jax.shard_map(body, mesh=mesh, in_specs=in_specs, out_specs=out_specs, check_vma=False)
```

```python
import jax
import jax.numpy as jnp
from jax import lax
from jax.experimental import pallas as pl
from jax.experimental.pallas import tpu as pltpu
from jax.sharding import PartitionSpec as P

AXES = ("span", "tm")
PLANES = 128
WINDOW = 2 * PLANES
DEV = 128
TM = 32
SPAN_DEV = 4
R_LOC = 16
A_LOC = 96
HALF = A_LOC // 2
A_ALL = SPAN_DEV * A_LOC
B = 192
SEND1 = 72
SEND2 = 40
PITCH = R_LOC + 1
PITCH2 = 8 + 1
PARTS = 4
F32 = jnp.float32
BF16 = jnp.bfloat16
MIB = 1024 * 1024
VMEM = pl.BlockSpec(memory_space=pltpu.VMEM)
SMEM = pl.BlockSpec(memory_space=pltpu.SMEM)
HBM = pl.BlockSpec(memory_space=pltpu.HBM)


def lanes(shape):
    return lax.broadcasted_iota(jnp.int32, shape, len(shape) - 1)


def deal_kernel(
    start_ref, owner_ref, core_ref, time_ref, span_ref, out_ref, tiles_ref, held, window, turned, stage, in_sem, time_sem, out_sem
):
    order = (2, 0, 1)
    ins = {c: pltpu.make_async_copy(core_ref.at[c], held.at[c], in_sem.at[c]) for c in order}
    start = start_ref[0]
    base = jnp.minimum(start // 128, (time_ref.shape[1] - WINDOW) // 128)
    window_in = pltpu.make_async_copy(
        time_ref.at[:, pl.ds(pl.multiple_of(base * 128, 128), WINDOW)], window, time_sem
    )
    window_in.start()
    for c in order:
        ins[c].start()
    eye = (
        lax.broadcasted_iota(jnp.int32, (B, B), 0) == lax.broadcasted_iota(jnp.int32, (B, B), 1)
    ).astype(BF16)
    lane = lanes((1, 128))
    for j in range(TM):
        owner = pl.multiple_of(owner_ref[j] * 8, 8)
        tiles_ref[pl.ds(owner, 8), :] = span_ref[8 * j : 8 * (j + 1), :]
    window_in.wait()
    rows = pltpu.roll(window[...].astype(F32), (WINDOW - (start - base * 128)) % WINDOW, 1)[:, :PLANES]
    rows = [pltpu.roll(rows, (A_LOC - 32 * q) % 128, 1) for q in range(4)]
    gap = jnp.zeros((128 - A_LOC, B), BF16)
    outs = []
    for c in order:
        ins[c].wait()
        for r in range(0, R_LOC, 2):
            x = jnp.concatenate([held[c, r], gap, held[c, r + 1], gap], axis=0)
            y = lax.dot_general(eye, x, (((1,), (1,)), ((), ())), preferred_element_type=F32)
            turned[pl.ds(r, B, PITCH), :] = y[:, :128]
            turned[pl.ds(r + 1, B, PITCH), :] = y[:, 128:]
        first = c * (B // 4)
        blocks = 48 if c < 2 else 32
        for b in range(4 * blocks):
            i, q = b // 4, b % 4
            block = jnp.where(lane < A_LOC, turned[pl.ds(PITCH * b, R_LOC), :], rows[q])
            stage[first + i, R_LOC * q : R_LOC * (q + 1), :] = block.astype(BF16)
        if c == 2:
            for j in range(64):
                low = turned[pl.ds(PITCH * (128 + j), 8), :]
                high = turned[pl.ds(PITCH * (128 + j) + 8, 8), :]
                at_0 = jnp.where(lane < HALF, low, pltpu.roll(high, HALF, 1))
                at_1 = jnp.where(lane < HALF, pltpu.roll(low, 128 - HALF, 1), high)
                stage[2 * j, 64:, :] = at_0.astype(BF16)
                stage[2 * j + 1, 64:, :] = at_1.astype(BF16)
        out = pltpu.make_async_copy(
            stage.at[pl.ds(first, blocks)], out_ref.at[pl.ds(first, blocks)], out_sem.at[c]
        )
        out.start()
        outs.append(out)
    for out in outs:
        out.wait()


def middle_kernel(held, span_ref, out_ref, span, firsts, span_sem):
    span_in = pltpu.make_async_copy(span_ref, span, span_sem)
    span_in.start()
    lane3 = lanes((1, 1, 128))
    lane = lanes((1, 128))
    odd = lax.rem(lax.axis_index("tm"), 2) == 1
    for g in range(SPAN_DEV):
        if g == 0:
            w = jnp.zeros((TM, R_LOC, 128), F32)
            for q in range(4):
                piece = held[:TM, R_LOC * q : R_LOC * (q + 1), :].astype(F32)
                piece = pltpu.roll(piece, (32 * q - A_LOC) % 128, 2)
                w = jnp.where((lane3 >= 32 * q) & (lane3 < 32 * q + 32), piece, w)
            whole = w.reshape(TM * R_LOC, 128).T.astype(BF16)
            low = w[:, :8].reshape(TM * 8, 128).T.astype(BF16)
            high = w[:, 8:].reshape(TM * 8, 128).T.astype(BF16)
        for q in range(4):
            x = held[TM * g : TM * (g + 1), R_LOC * q : R_LOC * (q + 1), :].reshape(TM * R_LOC, 128)
            firsts[q, g] = jnp.dot(whole, x, preferred_element_type=F32)
        x = held[TM * g : TM * (g + 1), 64:, :].astype(F32).reshape(TM * 8, 128).astype(BF16)
        fa = jnp.dot(low, x, preferred_element_type=F32)
        fb = jnp.dot(high, x, preferred_element_type=F32)
        even_sum = jnp.where(lane < HALF, fa + pltpu.roll(fb, 128 - HALF, 1), 0.0)
        odd_sum = jnp.where((lane >= HALF) & (lane < A_LOC), pltpu.roll(fa, HALF, 1) + fb, 0.0)
        firsts[4, g] = jnp.where(odd, odd_sum, even_sum)
    packed = []
    for q in range(5):
        f0, f1, f2, f3 = (firsts[q, g] for g in range(SPAN_DEV))
        tiles = (
            jnp.where(lane < 96, f0, pltpu.roll(f1, 96, 1)),
            jnp.where(lane < 64, pltpu.roll(f1, 96, 1), pltpu.roll(f2, 64, 1)),
            jnp.where(lane < 32, pltpu.roll(f2, 64, 1), pltpu.roll(f3, 32, 1)),
        )
        packed.append(jnp.concatenate(tiles, axis=1).astype(BF16))
    packed = jnp.concatenate(packed, axis=0)
    span_in.wait()
    for g in range(SPAN_DEV):
        z = lax.dot_general(
            span[TM * 8 * g : TM * 8 * (g + 1)],
            packed,
            (((1,), (1,)), ((), ())),
            preferred_element_type=F32,
        )
        for q in range(5):
            tile = z[:, 128 * q : 128 * (q + 1)].reshape(TM, 8, 128)
            out_ref[TM * g : TM * (g + 1), 8 * q : 8 * (q + 1), :] = tile.astype(BF16)


def height_kernel(held, height_ref, out_ref, height, wide, rows, stage, height_sem, out_sem):
    height_in = pltpu.make_async_copy(height_ref, height, height_sem)
    height_in.start()
    begins = (0, 48, 96)
    part = PLANES // PARTS
    outs = []
    for c in range(3):
        whole = B if c < 2 else 128
        for b in range(whole):
            source, q = begins[c] + b // 4, b % 4
            wide[c, pl.ds(PITCH2 * b, 8), :] = held[source, 8 * q : 8 * (q + 1), :].astype(F32)
        for b in range(whole, B):
            source = 2 * (b - 128)
            wide[c, pl.ds(PITCH2 * b, 8), :] = held[source, 32:, :].astype(F32) + held[source + 1, 32:, :].astype(F32)
        for s in range(8):
            x = wide.at[c][pl.ds(s, B, PITCH2), :].T
            rows.at[c, 0][pl.ds(s, PLANES, PITCH2), :] = x[:, :128]
            x = jnp.concatenate([x[:, 128:], jnp.zeros((PLANES, 256 - B), F32)], axis=1)
            rows.at[c, 1][pl.ds(s, PLANES, PITCH2), :] = x
        if c == 0:
            height_in.wait()
        for p in range(PARTS):
            x = [
                jnp.concatenate(
                    [rows[c, e, pl.ds(PITCH2 * t, 8), :] for t in range(part * p, part * (p + 1))], axis=0
                )
                for e in range(2)
            ]
            x = jnp.concatenate(x, axis=1)[:, :B].astype(BF16)
            y = jnp.dot(x, height[...], preferred_element_type=F32)
            at = pl.ds(part * p, part)
            stage[c, at] = y.reshape(part, 8, 512).astype(BF16)
            out = pltpu.make_async_copy(stage.at[c, at], out_ref.at[at, c], out_sem.at[PARTS * c + p])
            out.start()
            outs.append(out)
    for out in outs:
        out.wait()


def body(window_start, owner_map, core, span_factor, height_factor, time_factor):
    sent, tiles = pl.pallas_call(
        deal_kernel,
        out_shape=(
            jax.ShapeDtypeStruct((DEV, SEND1, 128), BF16),
            jax.ShapeDtypeStruct((8 * TM, A_ALL), BF16),
        ),
        in_specs=[SMEM, SMEM, HBM, HBM, VMEM],
        out_specs=(HBM, VMEM),
        scratch_shapes=[
            pltpu.VMEM((3, R_LOC, A_LOC, B), BF16),
            pltpu.VMEM((R_LOC, WINDOW), BF16),
            pltpu.VMEM((PITCH * B, 128), F32),
            pltpu.VMEM((DEV, SEND1, 128), BF16),
            pltpu.SemaphoreType.DMA((3,)),
            pltpu.SemaphoreType.DMA,
            pltpu.SemaphoreType.DMA((3,)),
        ],
        compiler_params=pltpu.CompilerParams(vmem_limit_bytes=60 * MIB),
        name="deal",
    )(window_start, owner_map, core, time_factor.T, span_factor)
    got = lax.all_to_all(sent, AXES, 0, 0, tiled=True)
    span = lax.all_gather(tiles, "span", axis=0, tiled=True)
    sent = pl.pallas_call(
        middle_kernel,
        out_shape=jax.ShapeDtypeStruct((DEV, SEND2, 128), BF16),
        in_specs=[VMEM, HBM],
        out_specs=VMEM,
        scratch_shapes=[
            pltpu.VMEM((8 * DEV, A_ALL), BF16),
            pltpu.VMEM((5, SPAN_DEV, PLANES, 128), F32),
            pltpu.SemaphoreType.DMA,
        ],
        compiler_params=pltpu.CompilerParams(vmem_limit_bytes=40 * MIB),
        name="middle",
    )(got, span)
    got = lax.all_to_all(sent, AXES, 0, 0, tiled=True)
    return pl.pallas_call(
        height_kernel,
        out_shape=jax.ShapeDtypeStruct((PLANES, 3, 8, 512), BF16),
        in_specs=[VMEM, HBM],
        out_specs=HBM,
        scratch_shapes=[
            pltpu.VMEM((B, 512), BF16),
            pltpu.VMEM((3, PITCH2 * B, 128), F32),
            pltpu.VMEM((3, 2, PITCH2 * PLANES, 128), F32),
            pltpu.VMEM((3, PLANES, 8, 512), BF16),
            pltpu.SemaphoreType.DMA,
            pltpu.SemaphoreType.DMA((3 * PARTS,)),
        ],
        compiler_params=pltpu.CompilerParams(vmem_limit_bytes=40 * MIB),
        name="height",
    )(got, height_factor.T)


def solution(mesh):
    in_specs = (P(), P(), P(None, "tm", "span", None), P("span", None), P(), P(None, "tm"))
    out_specs = P(None, None, ("span", "tm"), None)
    return jax.shard_map(body, mesh=mesh, in_specs=in_specs, out_specs=out_specs, check_vma=False)
```

```python
import jax
import jax.numpy as jnp
from jax import lax
from jax.experimental import pallas as pl
from jax.experimental.pallas import tpu as pltpu
from jax.sharding import PartitionSpec as P

AXES = ("span", "tm")
PLANES = 128
WINDOW = 2 * PLANES
DEV = 128
TM = 32
SPAN_DEV = 4
R_LOC = 16
A_LOC = 96
HALF = A_LOC // 2
A_ALL = SPAN_DEV * A_LOC
B = 192
SEND1 = 64
SEND2 = 40
PITCH = R_LOC + 1
PITCH2 = 8 + 1
PARTS = 4
F32 = jnp.float32
BF16 = jnp.bfloat16
MIB = 1024 * 1024
VMEM = pl.BlockSpec(memory_space=pltpu.VMEM)
SMEM = pl.BlockSpec(memory_space=pltpu.SMEM)
HBM = pl.BlockSpec(memory_space=pltpu.HBM)


def lanes(shape):
    return lax.broadcasted_iota(jnp.int32, shape, len(shape) - 1)


def deal_kernel(start_ref, core_ref, time_ref, out_ref, held, window, turned, start, in_sem, time_sem, start_sem):
    order = (2, 0, 1)
    ins = {c: pltpu.make_async_copy(core_ref.at[c], held.at[c], in_sem.at[c]) for c in order}
    start_in = pltpu.make_async_copy(start_ref, start, start_sem)
    start_in.start()
    for c in order:
        ins[c].start()
    start_in.wait()
    base = jnp.minimum(start[0] // 128, (time_ref.shape[1] - WINDOW) // 128)
    window_in = pltpu.make_async_copy(
        time_ref.at[:, pl.ds(pl.multiple_of(base * 128, 128), WINDOW)], window, time_sem
    )
    window_in.start()
    eye = (
        lax.broadcasted_iota(jnp.int32, (B, B), 0) == lax.broadcasted_iota(jnp.int32, (B, B), 1)
    ).astype(BF16)
    main = lanes((1, 128)) < A_LOC
    gap = jnp.zeros((128 - A_LOC, B), BF16)
    for c in order:
        ins[c].wait()
        for r in range(0, R_LOC, 2):
            x = jnp.concatenate([held[c, r], gap, held[c, r + 1], gap], axis=0)
            y = lax.dot_general(eye, x, (((1,), (1,)), ((), ())), preferred_element_type=F32)
            turned.at[c][pl.ds(r, B, PITCH), :] = y[:, :128]
            turned.at[c][pl.ds(r + 1, B, PITCH), :] = y[:, 128:]
        if c == order[0]:
            window_in.wait()
            quarter = (A_LOC - 32 * lax.axis_index("span") + 128) % 128
            rows = pltpu.roll(window[...].astype(F32), (WINDOW - (start[0] - base * 128)) % WINDOW, 1)[:, :PLANES]
            rows = pltpu.roll(rows, quarter, 1)
        for i in range(48 if c < 2 else 32):
            device = 48 * c + i
            half = turned[2, pl.ds(PITCH * (128 + device // 2), R_LOC), :]
            side = (
                pltpu.roll(half, A_LOC - HALF * (device % 2), 1),
                pltpu.roll(half, A_LOC - 32 - HALF * (device % 2), 1),
                rows,
                None,
            )
            for q in range(4):
                block = turned[c, pl.ds(PITCH * (4 * i + q), R_LOC), :]
                if side[q] is not None:
                    block = jnp.where(main, block, side[q])
                out_ref[device, R_LOC * q : R_LOC * (q + 1), :] = block.astype(BF16)


def middle_kernel(owner_ref, held, span_0, span_1, span_2, span_3, out_ref, span, firsts):
    mine = lax.axis_index("span")
    owners = [owner_ref[j] for j in range(TM)]
    for k, part in enumerate((span_0, span_1, span_2, span_3)):
        base = lax.bitwise_xor(mine, k) * TM
        for j in range(TM):
            at = pl.multiple_of((base + owners[j]) * 8, 8)
            span[pl.ds(at, 8), :] = part[8 * j : 8 * (j + 1), :].astype(F32)
    lane3 = lanes((1, 1, 128))
    lane = lanes((1, 128))
    w = jnp.zeros((TM, R_LOC, 128), F32)
    for g in range(SPAN_DEV):
        piece = held[TM * g : TM * (g + 1), 2 * R_LOC : 3 * R_LOC, :].astype(F32)
        piece = pltpu.roll(piece, (32 * g - A_LOC) % 128, 2)
        w = jnp.where((lane3 >= 32 * g) & (lane3 < 32 * g + 32), piece, w)
    w = w.reshape(TM * R_LOC, 128).T.astype(BF16)
    low = HALF * lax.rem(lax.axis_index("tm"), 2)
    for g in range(SPAN_DEV):
        f = []
        for q in range(4):
            x = held[TM * g : TM * (g + 1), R_LOC * q : R_LOC * (q + 1), :].reshape(TM * R_LOC, 128)
            f.append(jnp.dot(w, x, preferred_element_type=F32))
            firsts[q, g] = f[q]
        half = jnp.where(lane < low + 32, pltpu.roll(f[0], low + 32, 1), pltpu.roll(f[1], low + 64, 1))
        firsts[4, g] = jnp.where((lane >= low) & (lane < low + HALF), half, 0.0)
    packed = []
    for q in range(5):
        f0, f1, f2, f3 = (firsts[q, g] for g in range(SPAN_DEV))
        tiles = (
            jnp.where(lane < 96, f0, pltpu.roll(f1, 96, 1)),
            jnp.where(lane < 64, pltpu.roll(f1, 96, 1), pltpu.roll(f2, 64, 1)),
            jnp.where(lane < 32, pltpu.roll(f2, 64, 1), pltpu.roll(f3, 32, 1)),
        )
        packed.append(jnp.concatenate(tiles, axis=1).astype(BF16))
    packed = jnp.concatenate(packed, axis=0)
    for g in range(SPAN_DEV):
        z = lax.dot_general(
            span[TM * 8 * g : TM * 8 * (g + 1)].astype(BF16),
            packed,
            (((1,), (1,)), ((), ())),
            preferred_element_type=F32,
        )
        for q in range(5):
            tile = z[:, 128 * q : 128 * (q + 1)].reshape(TM, 8, 128)
            out_ref[TM * g : TM * (g + 1), 8 * q : 8 * (q + 1), :] = tile.astype(BF16)


def height_kernel(held, height_ref, out_ref, height, wide, rows, stage, height_sem, out_sem):
    height_in = pltpu.make_async_copy(height_ref, height, height_sem)
    height_in.start()
    begins = (0, 48, 96)
    part = PLANES // PARTS
    outs = []
    for c in range(3):
        whole = B if c < 2 else 128
        for b in range(whole):
            source, q = begins[c] + b // 4, b % 4
            wide[c, pl.ds(PITCH2 * b, 8), :] = held[source, 8 * q : 8 * (q + 1), :].astype(F32)
        for b in range(whole, B):
            source = 2 * (b - 128)
            wide[c, pl.ds(PITCH2 * b, 8), :] = held[source, 32:, :].astype(F32) + held[source + 1, 32:, :].astype(F32)
        for s in range(8):
            x = wide.at[c][pl.ds(s, B, PITCH2), :].T
            rows.at[c, 0][pl.ds(s, PLANES, PITCH2), :] = x[:, :128]
            x = jnp.concatenate([x[:, 128:], jnp.zeros((PLANES, 256 - B), F32)], axis=1)
            rows.at[c, 1][pl.ds(s, PLANES, PITCH2), :] = x
        if c == 0:
            height_in.wait()
        for p in range(PARTS):
            x = [
                jnp.concatenate(
                    [rows[c, e, pl.ds(PITCH2 * t, 8), :] for t in range(part * p, part * (p + 1))], axis=0
                )
                for e in range(2)
            ]
            x = jnp.concatenate(x, axis=1)[:, :B].astype(BF16)
            y = jnp.dot(x, height[...], preferred_element_type=F32)
            at = pl.ds(part * p, part)
            stage[c, at] = y.reshape(part, 8, 512).astype(BF16)
            out = pltpu.make_async_copy(stage.at[c, at], out_ref.at[at, c], out_sem.at[PARTS * c + p])
            out.start()
            outs.append(out)
    for out in outs:
        out.wait()


def moves(step, flip):
    pairs = []
    for device in range(DEV):
        low, core, z, high, x = device // 64, device // 32 % 2, device // 8 % 4, device // 4 % 2, device % 4
        y = (2 * high + low + step) % 4
        pairs.append((device, ((y % 2 * 2 + (core ^ flip)) * 4 + z) * 8 + y // 2 * 4 + x))
    return pairs


def body(window_start, owner_map, core, span_factor, height_factor, time_factor):
    spans = [lax.ppermute(span_factor, AXES, moves(*way)) for way in ((-1, 1), (1, 0), (0, 1))]
    spans = [span_factor] + spans[::-1]
    sent = pl.pallas_call(
        deal_kernel,
        out_shape=pltpu.VMEM((DEV, SEND1, 128), BF16),
        in_specs=[HBM, HBM, HBM],
        out_specs=VMEM,
        scratch_shapes=[
            pltpu.VMEM((3, R_LOC, A_LOC, B), BF16),
            pltpu.VMEM((R_LOC, WINDOW), BF16),
            pltpu.VMEM((3, PITCH * B, 128), F32),
            pltpu.SMEM((1,), jnp.int32),
            pltpu.SemaphoreType.DMA((3,)),
            pltpu.SemaphoreType.DMA,
            pltpu.SemaphoreType.DMA,
        ],
        compiler_params=pltpu.CompilerParams(vmem_limit_bytes=60 * MIB),
        cost_estimate=pl.CostEstimate(flops=4_000_000_000, bytes_accessed=5_000_000, transcendentals=0),
        name="deal",
    )(window_start, core, time_factor.T)
    sent, *spans = lax.optimization_barrier((sent, *spans))
    got = lax.all_to_all(sent, AXES, 0, 0, tiled=True)
    sent = pl.pallas_call(
        middle_kernel,
        out_shape=jax.ShapeDtypeStruct((DEV, SEND2, 128), BF16),
        in_specs=[SMEM] + [VMEM] * 5,
        out_specs=VMEM,
        scratch_shapes=[
            pltpu.VMEM((8 * DEV, A_ALL), F32),
            pltpu.VMEM((5, SPAN_DEV, PLANES, 128), F32),
        ],
        compiler_params=pltpu.CompilerParams(vmem_limit_bytes=40 * MIB),
        name="middle",
    )(owner_map, got, *spans)
    got = lax.all_to_all(sent, AXES, 0, 0, tiled=True)
    return pl.pallas_call(
        height_kernel,
        out_shape=jax.ShapeDtypeStruct((PLANES, 3, 8, 512), BF16),
        in_specs=[VMEM, HBM],
        out_specs=HBM,
        scratch_shapes=[
            pltpu.VMEM((B, 512), BF16),
            pltpu.VMEM((3, PITCH2 * B, 128), F32),
            pltpu.VMEM((3, 2, PITCH2 * PLANES, 128), F32),
            pltpu.VMEM((3, PLANES, 8, 512), BF16),
            pltpu.SemaphoreType.DMA,
            pltpu.SemaphoreType.DMA((3 * PARTS,)),
        ],
        compiler_params=pltpu.CompilerParams(vmem_limit_bytes=40 * MIB),
        name="height",
    )(got, height_factor.T)


def solution(mesh):
    in_specs = (P(), P(), P(None, "tm", "span", None), P("span", None), P(), P(None, "tm"))
    out_specs = P(None, None, ("span", "tm"), None)
    return jax.shard_map(body, mesh=mesh, in_specs=in_specs, out_specs=out_specs, check_vma=False)
```

```python
import jax
import jax.numpy as jnp
from jax import lax
from jax.experimental import pallas as pl
from jax.experimental.pallas import tpu as pltpu
from jax.sharding import PartitionSpec as P

AXES = ("span", "tm")
PLANES = 128
WINDOW = 2 * PLANES
DEV = 128
TM = 32
SPAN_DEV = 4
R_LOC = 16
A_LOC = 96
HALF = A_LOC // 2
A_ALL = SPAN_DEV * A_LOC
B = 192
SEND1 = 64
SEND2 = 40
PITCH = R_LOC + 1
PITCH2 = 8 + 1
PARTS = 4
F32 = jnp.float32
BF16 = jnp.bfloat16
MIB = 1024 * 1024
VMEM = pl.BlockSpec(memory_space=pltpu.VMEM)
SMEM = pl.BlockSpec(memory_space=pltpu.SMEM)
HBM = pl.BlockSpec(memory_space=pltpu.HBM)


def lanes(shape):
    return lax.broadcasted_iota(jnp.int32, shape, len(shape) - 1)


def deal_kernel(
    start_ref, core_ref, time_ref, out_ref, held, window, turned, stage, start, in_sem, time_sem, start_sem, out_sem
):
    order = (2, 0, 1)
    ins = {c: pltpu.make_async_copy(core_ref.at[c], held.at[c], in_sem.at[c]) for c in order}
    start_in = pltpu.make_async_copy(start_ref, start, start_sem)
    start_in.start()
    for c in order:
        ins[c].start()
    start_in.wait()
    base = jnp.minimum(start[0] // 128, (time_ref.shape[1] - WINDOW) // 128)
    window_in = pltpu.make_async_copy(
        time_ref.at[:, pl.ds(pl.multiple_of(base * 128, 128), WINDOW)], window, time_sem
    )
    window_in.start()
    eye = (
        lax.broadcasted_iota(jnp.int32, (B, B), 0) == lax.broadcasted_iota(jnp.int32, (B, B), 1)
    ).astype(BF16)
    main = lanes((1, 128)) < A_LOC
    gap = jnp.zeros((128 - A_LOC, B), BF16)
    outs = []
    for c in order:
        ins[c].wait()
        for r in range(0, R_LOC, 2):
            x = jnp.concatenate([held[c, r], gap, held[c, r + 1], gap], axis=0)
            y = lax.dot_general(eye, x, (((1,), (1,)), ((), ())), preferred_element_type=F32)
            turned.at[c][pl.ds(r, B, PITCH), :] = y[:, :128]
            turned.at[c][pl.ds(r + 1, B, PITCH), :] = y[:, 128:]
        if c == order[0]:
            window_in.wait()
            quarter = (A_LOC - 32 * lax.axis_index("span") + 128) % 128
            rows = pltpu.roll(window[...].astype(F32), (WINDOW - (start[0] - base * 128)) % WINDOW, 1)[:, :PLANES]
            rows = pltpu.roll(rows, quarter, 1)
        for i in range(48 if c < 2 else 32):
            device = 48 * c + i
            half = turned[2, pl.ds(PITCH * (128 + device // 2), R_LOC), :]
            side = (
                pltpu.roll(half, A_LOC - HALF * (device % 2), 1),
                pltpu.roll(half, A_LOC - 32 - HALF * (device % 2), 1),
                rows,
                None,
            )
            for q in range(4):
                block = turned[c, pl.ds(PITCH * (4 * i + q), R_LOC), :]
                if side[q] is not None:
                    block = jnp.where(main, block, side[q])
                stage[device, R_LOC * q : R_LOC * (q + 1), :] = block.astype(BF16)
        at = pl.ds(48 * c, 48 if c < 2 else 32)
        outs.append(pltpu.make_async_copy(stage.at[at], out_ref.at[at], out_sem.at[c]))
        outs[-1].start()
    for out in outs:
        out.wait()


def middle_kernel(owner_ref, held, span_0, span_1, span_2, span_3, out_ref, span, firsts):
    mine = lax.axis_index("span")
    owners = [owner_ref[j] for j in range(TM)]
    for k, part in enumerate((span_0, span_1, span_2, span_3)):
        base = lax.bitwise_xor(mine, k) * TM
        for j in range(TM):
            at = pl.multiple_of((base + owners[j]) * 8, 8)
            span[pl.ds(at, 8), :] = part[8 * j : 8 * (j + 1), :].astype(F32)
    lane3 = lanes((1, 1, 128))
    lane = lanes((1, 128))
    w = jnp.zeros((TM, R_LOC, 128), F32)
    for g in range(SPAN_DEV):
        piece = held[TM * g : TM * (g + 1), 2 * R_LOC : 3 * R_LOC, :].astype(F32)
        piece = pltpu.roll(piece, (32 * g - A_LOC) % 128, 2)
        w = jnp.where((lane3 >= 32 * g) & (lane3 < 32 * g + 32), piece, w)
    w = w.reshape(TM * R_LOC, 128).T.astype(BF16)
    low = HALF * lax.rem(lax.axis_index("tm"), 2)
    for g in range(SPAN_DEV):
        f = []
        for q in (0, 2):
            x = [
                held[TM * g : TM * (g + 1), R_LOC * p : R_LOC * (p + 1), :].reshape(TM * R_LOC, 128)
                for p in (q, q + 1)
            ]
            y = jnp.dot(w, jnp.concatenate(x, axis=1), preferred_element_type=F32)
            f += [y[:, :128], y[:, 128:]]
        for q in range(4):
            firsts[q, g] = f[q]
        half = jnp.where(lane < low + 32, pltpu.roll(f[0], low + 32, 1), pltpu.roll(f[1], low + 64, 1))
        firsts[4, g] = jnp.where((lane >= low) & (lane < low + HALF), half, 0.0)
    packed = []
    for q in range(5):
        f0, f1, f2, f3 = (firsts[q, g] for g in range(SPAN_DEV))
        tiles = (
            jnp.where(lane < 96, f0, pltpu.roll(f1, 96, 1)),
            jnp.where(lane < 64, pltpu.roll(f1, 96, 1), pltpu.roll(f2, 64, 1)),
            jnp.where(lane < 32, pltpu.roll(f2, 64, 1), pltpu.roll(f3, 32, 1)),
        )
        packed.append(jnp.concatenate(tiles, axis=1).astype(BF16))
    packed = jnp.concatenate(packed, axis=0)
    z = lax.dot_general(
        span[...].astype(BF16), packed, (((1,), (1,)), ((), ())), preferred_element_type=F32
    )
    for q in range(5):
        out_ref[:, 8 * q : 8 * (q + 1), :] = z[:, 128 * q : 128 * (q + 1)].reshape(DEV, 8, 128).astype(BF16)


def height_kernel(held, height_ref, out_ref, height, wide, rows, stage, height_sem, out_sem):
    height_in = pltpu.make_async_copy(height_ref, height, height_sem)
    height_in.start()
    begins = (0, 48, 96)
    part = PLANES // PARTS
    outs = []
    for c in range(3):
        whole = B if c < 2 else 128
        for b in range(whole):
            source, q = begins[c] + b // 4, b % 4
            wide[c, pl.ds(PITCH2 * b, 8), :] = held[source, 8 * q : 8 * (q + 1), :].astype(F32)
        for b in range(whole, B):
            source = 2 * (b - 128)
            wide[c, pl.ds(PITCH2 * b, 8), :] = held[source, 32:, :].astype(F32) + held[source + 1, 32:, :].astype(F32)
        for s in range(8):
            x = wide.at[c][pl.ds(s, B, PITCH2), :].T
            rows.at[c, 0][pl.ds(s, PLANES, PITCH2), :] = x[:, :128]
            x = jnp.concatenate([x[:, 128:], jnp.zeros((PLANES, 256 - B), F32)], axis=1)
            rows.at[c, 1][pl.ds(s, PLANES, PITCH2), :] = x
        if c == 0:
            height_in.wait()
        for p in range(PARTS):
            x = [
                jnp.concatenate(
                    [rows[c, e, pl.ds(PITCH2 * t, 8), :] for t in range(part * p, part * (p + 1))], axis=0
                )
                for e in range(2)
            ]
            x = jnp.concatenate(x, axis=1)[:, :B].astype(BF16)
            y = jnp.dot(x, height[...], preferred_element_type=F32)
            at = pl.ds(part * p, part)
            stage[c, at] = y.reshape(part, 8, 512).astype(BF16)
            out = pltpu.make_async_copy(stage.at[c, at], out_ref.at[at, c], out_sem.at[PARTS * c + p])
            out.start()
            outs.append(out)
    for out in outs:
        out.wait()


def moves(step, flip):
    pairs = []
    for device in range(DEV):
        low, core, z, high, x = device // 64, device // 32 % 2, device // 8 % 4, device // 4 % 2, device % 4
        y = (2 * high + low + step) % 4
        pairs.append((device, ((y % 2 * 2 + (core ^ flip)) * 4 + z) * 8 + y // 2 * 4 + x))
    return pairs


def body(window_start, owner_map, core, span_factor, height_factor, time_factor):
    across = lax.ppermute(span_factor, AXES, moves(1, 0))
    sent = pl.pallas_call(
        deal_kernel,
        out_shape=jax.ShapeDtypeStruct((DEV, SEND1, 128), BF16),
        in_specs=[HBM, HBM, HBM],
        out_specs=HBM,
        scratch_shapes=[
            pltpu.VMEM((3, R_LOC, A_LOC, B), BF16),
            pltpu.VMEM((R_LOC, WINDOW), BF16),
            pltpu.VMEM((3, PITCH * B, 128), F32),
            pltpu.VMEM((DEV, SEND1, 128), BF16),
            pltpu.SMEM((1,), jnp.int32),
            pltpu.SemaphoreType.DMA((3,)),
            pltpu.SemaphoreType.DMA,
            pltpu.SemaphoreType.DMA,
            pltpu.SemaphoreType.DMA((3,)),
        ],
        compiler_params=pltpu.CompilerParams(vmem_limit_bytes=60 * MIB),
        cost_estimate=pl.CostEstimate(flops=4_000_000_000, bytes_accessed=5_000_000, transcendentals=0),
        name="deal",
    )(window_start, core, time_factor.T)
    sent, span_factor, across = lax.optimization_barrier((sent, span_factor, across))
    spans = [span_factor, lax.ppermute(span_factor, AXES, moves(0, 1)), across, lax.ppermute(across, AXES, moves(0, 1))]
    got = lax.all_to_all(sent, AXES, 0, 0, tiled=True)
    sent = pl.pallas_call(
        middle_kernel,
        out_shape=jax.ShapeDtypeStruct((DEV, SEND2, 128), BF16),
        in_specs=[SMEM] + [VMEM] * 5,
        out_specs=VMEM,
        scratch_shapes=[
            pltpu.VMEM((8 * DEV, A_ALL), F32),
            pltpu.VMEM((5, SPAN_DEV, PLANES, 128), F32),
        ],
        compiler_params=pltpu.CompilerParams(vmem_limit_bytes=40 * MIB),
        name="middle",
    )(owner_map, got, *spans)
    got = lax.all_to_all(sent, AXES, 0, 0, tiled=True)
    return pl.pallas_call(
        height_kernel,
        out_shape=jax.ShapeDtypeStruct((PLANES, 3, 8, 512), BF16),
        in_specs=[VMEM, HBM],
        out_specs=HBM,
        scratch_shapes=[
            pltpu.VMEM((B, 512), BF16),
            pltpu.VMEM((3, PITCH2 * B, 128), F32),
            pltpu.VMEM((3, 2, PITCH2 * PLANES, 128), F32),
            pltpu.VMEM((3, PLANES, 8, 512), BF16),
            pltpu.SemaphoreType.DMA,
            pltpu.SemaphoreType.DMA((3 * PARTS,)),
        ],
        compiler_params=pltpu.CompilerParams(vmem_limit_bytes=40 * MIB),
        name="height",
    )(got, height_factor.T)


def solution(mesh):
    in_specs = (P(), P(), P(None, "tm", "span", None), P("span", None), P(), P(None, "tm"))
    out_specs = P(None, None, ("span", "tm"), None)
    return jax.shard_map(body, mesh=mesh, in_specs=in_specs, out_specs=out_specs, check_vma=False)
```

```python
import jax
import jax.numpy as jnp
from jax import lax
from jax.experimental import pallas as pl
from jax.experimental.pallas import tpu as pltpu
from jax.sharding import PartitionSpec as P

AXES = ("span", "tm")
PLANES = 128
WINDOW = 2 * PLANES
DEV = 128
TM = 32
SPAN_DEV = 4
R_LOC = 16
A_LOC = 96
HALF = A_LOC // 2
A_ALL = SPAN_DEV * A_LOC
B = 192
SEND1 = 64
SEND2 = 40
PITCH = R_LOC + 1
PITCH2 = 8 + 1
PARTS = 4
F32 = jnp.float32
BF16 = jnp.bfloat16
MIB = 1024 * 1024
VMEM = pl.BlockSpec(memory_space=pltpu.VMEM)
SMEM = pl.BlockSpec(memory_space=pltpu.SMEM)
HBM = pl.BlockSpec(memory_space=pltpu.HBM)


def lanes(shape):
    return lax.broadcasted_iota(jnp.int32, shape, len(shape) - 1)


def deal_kernel(
    start_ref, core_ref, time_ref, out_ref, held, window, turned, stage, start, in_sem, time_sem, start_sem, out_sem
):
    order = (2, 0, 1)
    ins = {c: pltpu.make_async_copy(core_ref.at[c], held.at[c], in_sem.at[c]) for c in order}
    start_in = pltpu.make_async_copy(start_ref, start, start_sem)
    start_in.start()
    for c in order:
        ins[c].start()
    start_in.wait()
    base = jnp.minimum(start[0] // 128, (time_ref.shape[1] - WINDOW) // 128)
    window_in = pltpu.make_async_copy(
        time_ref.at[:, pl.ds(pl.multiple_of(base * 128, 128), WINDOW)], window, time_sem
    )
    window_in.start()
    eye = (
        lax.broadcasted_iota(jnp.int32, (B, B), 0) == lax.broadcasted_iota(jnp.int32, (B, B), 1)
    ).astype(BF16)
    main = lanes((1, 128)) < A_LOC
    gap = jnp.zeros((128 - A_LOC, B), BF16)
    outs = []
    for c in order:
        ins[c].wait()
        for r in range(0, R_LOC, 2):
            x = jnp.concatenate([held[c, r], gap, held[c, r + 1], gap], axis=0)
            y = lax.dot_general(eye, x, (((1,), (1,)), ((), ())), preferred_element_type=F32)
            turned.at[c][pl.ds(r, B, PITCH), :] = y[:, :128]
            turned.at[c][pl.ds(r + 1, B, PITCH), :] = y[:, 128:]
        if c == order[0]:
            window_in.wait()
            quarter = (A_LOC - 32 * lax.axis_index("span") + 128) % 128
            rows = pltpu.roll(window[...].astype(F32), (WINDOW - (start[0] - base * 128)) % WINDOW, 1)[:, :PLANES]
            rows = pltpu.roll(rows, quarter, 1)
        for i in range(48 if c < 2 else 32):
            device = 48 * c + i
            half = turned[2, pl.ds(PITCH * (128 + device // 2), R_LOC), :]
            side = (
                pltpu.roll(half, A_LOC - HALF * (device % 2), 1),
                pltpu.roll(half, A_LOC - 32 - HALF * (device % 2), 1),
                rows,
                None,
            )
            for q in range(4):
                block = turned[c, pl.ds(PITCH * (4 * i + q), R_LOC), :]
                if side[q] is not None:
                    block = jnp.where(main, block, side[q])
                stage[device, R_LOC * q : R_LOC * (q + 1), :] = block.astype(BF16)
        at = pl.ds(48 * c, 48 if c < 2 else 32)
        outs.append(pltpu.make_async_copy(stage.at[at], out_ref.at[at], out_sem.at[c]))
        outs[-1].start()
    for out in outs:
        out.wait()


def middle_kernel(owner_ref, held, span_0, span_1, span_2, span_3, out_ref, span, firsts):
    mine = lax.axis_index("span")
    owners = [owner_ref[j] for j in range(TM)]
    for k, part in enumerate((span_0, span_1, span_2, span_3)):
        base = lax.bitwise_xor(mine, k) * TM
        for j in range(TM):
            at = pl.multiple_of((base + owners[j]) * 8, 8)
            span[pl.ds(at, 8), :] = part[8 * j : 8 * (j + 1), :].astype(F32)
    lane3 = lanes((1, 1, 128))
    lane = lanes((1, 128))
    w = jnp.zeros((TM, R_LOC, 128), F32)
    for g in range(SPAN_DEV):
        piece = held[TM * g : TM * (g + 1), 2 * R_LOC : 3 * R_LOC, :].astype(F32)
        piece = pltpu.roll(piece, (32 * g - A_LOC) % 128, 2)
        w = jnp.where((lane3 >= 32 * g) & (lane3 < 32 * g + 32), piece, w)
    w = w.reshape(TM * R_LOC, 128).T.astype(BF16)
    low = HALF * lax.rem(lax.axis_index("tm"), 2)
    for g in range(SPAN_DEV):
        f = []
        for q in (0, 2):
            x = [
                held[TM * g : TM * (g + 1), R_LOC * p : R_LOC * (p + 1), :].reshape(TM * R_LOC, 128)
                for p in (q, q + 1)
            ]
            y = jnp.dot(w, jnp.concatenate(x, axis=1), preferred_element_type=F32)
            f += [y[:, :128], y[:, 128:]]
        for q in range(4):
            firsts[q, g] = f[q]
        half = jnp.where(lane < low + 32, pltpu.roll(f[0], low + 32, 1), pltpu.roll(f[1], low + 64, 1))
        firsts[4, g] = jnp.where((lane >= low) & (lane < low + HALF), half, 0.0)
    packed = []
    for q in range(5):
        f0, f1, f2, f3 = (firsts[q, g] for g in range(SPAN_DEV))
        tiles = (
            jnp.where(lane < 96, f0, pltpu.roll(f1, 96, 1)),
            jnp.where(lane < 64, pltpu.roll(f1, 96, 1), pltpu.roll(f2, 64, 1)),
            jnp.where(lane < 32, pltpu.roll(f2, 64, 1), pltpu.roll(f3, 32, 1)),
        )
        packed.append(jnp.concatenate(tiles, axis=1).astype(BF16))
    packed = jnp.concatenate(packed, axis=0)
    z = lax.dot_general(
        span[...].astype(BF16), packed, (((1,), (1,)), ((), ())), preferred_element_type=F32
    )
    for q in range(5):
        out_ref[:, 8 * q : 8 * (q + 1), :] = z[:, 128 * q : 128 * (q + 1)].reshape(DEV, 8, 128).astype(BF16)


def height_kernel(held, height_ref, out_ref, height, wide, rows, stage, height_sem, out_sem):
    height_in = pltpu.make_async_copy(height_ref, height, height_sem)
    height_in.start()
    begins = (0, 48, 96)
    part = PLANES // PARTS
    outs = []
    for c in range(3):
        whole = B if c < 2 else 128
        for b in range(whole):
            source, q = begins[c] + b // 4, b % 4
            wide[c, pl.ds(PITCH2 * b, 8), :] = held[source, 8 * q : 8 * (q + 1), :].astype(F32)
        for b in range(whole, B):
            source = 2 * (b - 128)
            wide[c, pl.ds(PITCH2 * b, 8), :] = held[source, 32:, :].astype(F32) + held[source + 1, 32:, :].astype(F32)
        for s in range(8):
            x = wide.at[c][pl.ds(s, B, PITCH2), :].T
            rows.at[c, 0][pl.ds(s, PLANES, PITCH2), :] = x[:, :128]
            x = jnp.concatenate([x[:, 128:], jnp.zeros((PLANES, 256 - B), F32)], axis=1)
            rows.at[c, 1][pl.ds(s, PLANES, PITCH2), :] = x
        if c == 0:
            height_in.wait()
        for p in range(PARTS):
            x = [
                jnp.concatenate(
                    [rows[c, e, pl.ds(PITCH2 * t, 8), :] for t in range(part * p, part * (p + 1))], axis=0
                )
                for e in range(2)
            ]
            x = jnp.concatenate(x, axis=1)[:, :B].astype(BF16)
            y = jnp.dot(x, height[...], preferred_element_type=F32)
            at = pl.ds(part * p, part)
            stage[c, at] = y.reshape(part, 8, 512).astype(BF16)
            out = pltpu.make_async_copy(stage.at[c, at], out_ref.at[at, c], out_sem.at[PARTS * c + p])
            out.start()
            outs.append(out)
    for out in outs:
        out.wait()


def moves(step, flip):
    pairs = []
    for device in range(DEV):
        low, core, z, high, x = device // 64, device // 32 % 2, device // 8 % 4, device // 4 % 2, device % 4
        y = (2 * high + low + (-step if core else step)) % 4
        pairs.append((device, ((y % 2 * 2 + (core ^ flip)) * 4 + z) * 8 + y // 2 * 4 + x))
    return pairs


def body(window_start, owner_map, core, span_factor, height_factor, time_factor):
    across = lax.ppermute(span_factor, AXES, moves(1, 0))
    sent = pl.pallas_call(
        deal_kernel,
        out_shape=jax.ShapeDtypeStruct((DEV, SEND1, 128), BF16),
        in_specs=[HBM, HBM, HBM],
        out_specs=HBM,
        scratch_shapes=[
            pltpu.VMEM((3, R_LOC, A_LOC, B), BF16),
            pltpu.VMEM((R_LOC, WINDOW), BF16),
            pltpu.VMEM((3, PITCH * B, 128), F32),
            pltpu.VMEM((DEV, SEND1, 128), BF16),
            pltpu.SMEM((1,), jnp.int32),
            pltpu.SemaphoreType.DMA((3,)),
            pltpu.SemaphoreType.DMA,
            pltpu.SemaphoreType.DMA,
            pltpu.SemaphoreType.DMA((3,)),
        ],
        compiler_params=pltpu.CompilerParams(vmem_limit_bytes=60 * MIB),
        cost_estimate=pl.CostEstimate(flops=4_000_000_000, bytes_accessed=5_000_000, transcendentals=0),
        name="deal",
    )(window_start, core, time_factor.T)
    sent, span_factor, across = lax.optimization_barrier((sent, span_factor, across))
    spans = [span_factor, lax.ppermute(span_factor, AXES, moves(0, 1)), across, lax.ppermute(across, AXES, moves(0, 1))]
    got = lax.all_to_all(sent, AXES, 0, 0, tiled=True)
    sent = pl.pallas_call(
        middle_kernel,
        out_shape=jax.ShapeDtypeStruct((DEV, SEND2, 128), BF16),
        in_specs=[SMEM] + [VMEM] * 5,
        out_specs=VMEM,
        scratch_shapes=[
            pltpu.VMEM((8 * DEV, A_ALL), F32),
            pltpu.VMEM((5, SPAN_DEV, PLANES, 128), F32),
        ],
        compiler_params=pltpu.CompilerParams(vmem_limit_bytes=40 * MIB),
        name="middle",
    )(owner_map, got, *spans)
    got = lax.all_to_all(sent, AXES, 0, 0, tiled=True)
    return pl.pallas_call(
        height_kernel,
        out_shape=jax.ShapeDtypeStruct((PLANES, 3, 8, 512), BF16),
        in_specs=[VMEM, HBM],
        out_specs=HBM,
        scratch_shapes=[
            pltpu.VMEM((B, 512), BF16),
            pltpu.VMEM((3, PITCH2 * B, 128), F32),
            pltpu.VMEM((3, 2, PITCH2 * PLANES, 128), F32),
            pltpu.VMEM((3, PLANES, 8, 512), BF16),
            pltpu.SemaphoreType.DMA,
            pltpu.SemaphoreType.DMA((3 * PARTS,)),
        ],
        compiler_params=pltpu.CompilerParams(vmem_limit_bytes=40 * MIB),
        name="height",
    )(got, height_factor.T)


def solution(mesh):
    in_specs = (P(), P(), P(None, "tm", "span", None), P("span", None), P(), P(None, "tm"))
    out_specs = P(None, None, ("span", "tm"), None)
    return jax.shard_map(body, mesh=mesh, in_specs=in_specs, out_specs=out_specs, check_vma=False)
```
